32 devices in a mesh: row: 4 (over y, x), col: 8 (over z, core).
Axes of the slice: x: 2, y: 2, z: 4, core: 2. Of those that a mesh axis runs over, the one named last changes fastest.
Arguments:
- gradient: bfloat16 [3072, 8192], P('row', 'col'), may hold values from -6 to 6
- left_basis: bfloat16 [3072, 3072], P('row'), may hold values from -0.109375 to 0.109375
- right_basis: bfloat16 [8192, 8192], P('col'), may hold values from -0.0625 to 0.0625
- first_moment: float32 [3072, 8192], P('row', 'col'), may hold values from -6 to 6
- second_moment: float32 [3072, 8192], P('row', 'col'), may hold values from 0.1 to 4
Outputs:
- new_first: float32 [3072, 8192], P('row', 'col')
- new_second: float32 [3072, 8192], P('row', 'col')
- update: float32 [3072, 8192], P('row', 'col')
The draws below stay inside these ranges and needn't reach their ends.
All inputs are finite; a program needn't handle non-finite values.
Results may differ from the reference program's by a relative error of at most 0.0095.
Values may be sent and summed in bfloat16 or wider, within the bound.
No kernel may reach another device: no remote copies, remote signals or barrier semaphores. Data moves between devices by JAX's collectives and lax.ppermute only.
A program may use at most 128 MiB of HBM per device.

```python
import math
import jax
import jax.numpy as jnp
from jax import lax

M = 3072
N = 8192
N_COL = 8


def shard_levels(own_key, dims, cuts, low, largest):
    loudness = 1.0
    for axis_at, shards_of in cuts:
        heights = jax.random.uniform(jax.random.fold_in(jax.random.fold_in(own_key, 6), axis_at), (shards_of,), jnp.float32, low / len(cuts), largest / len(cuts))
        loudness = loudness * jnp.repeat(jnp.exp(heights), dims[axis_at] // shards_of).reshape((-1,) + (1,) * (len(dims) - 1 - axis_at))
    return loudness


def centred(key, extent, scale, limit, cuts=(), dtype=jnp.bfloat16):
    factor_of = shard_levels(key, extent, cuts, -0.22, 0.18) if cuts else 1.0
    result = jax.random.normal(key, extent, jnp.float32) * scale * factor_of
    return jnp.minimum(jnp.maximum(result, -limit), limit).astype(dtype)


def setup_inputs(seed: int = 0) -> dict:
    splits = jax.random.split(jax.random.key(seed), 6)
    return {
        "gradient": centred(splits[0], (M, N), 1.0, 6.0, ((0, 4), (1, 8))),
        "left_basis": centred(splits[1], (M, M), M ** -0.5, 0.109375, ((0, 4),)),
        "right_basis": centred(splits[2], (N, N), N ** -0.5, 0.0625, ((0, 8),)),
        "first_moment": centred(splits[3], (M, N), 1.0, 6.0, ((0, 4), (1, 8)), jnp.float32),
        "second_moment": jnp.clip(jnp.exp(math.log(4.0) - 3.6888794 * jax.random.uniform(splits[4], (M, N), jnp.float32) ** shard_levels(splits[4], (M, N), ((0, 4), (1, 8)), -0.2, 0.2)), 0.1, 4.0),
    }


def reference(gradient, left_basis, right_basis, first_moment, second_moment):
    width = N // N_COL
    grad_blocks = gradient.reshape(M, N_COL, width).transpose(1, 0, 2)
    basis_blocks = right_basis.reshape(N_COL, width, N)

    def add_block(total, pair):
        partial_value = jnp.dot(pair[0], pair[1], preferred_element_type=jnp.float32).astype(jnp.bfloat16)
        partial_value = lax.optimization_barrier(partial_value)
        return (total + partial_value.astype(jnp.float32), None)
    summed, _ = lax.scan(add_block, jnp.zeros((M, N), jnp.float32), (grad_blocks, basis_blocks))
    right_rotated = summed.astype(jnp.bfloat16)
    rotated = jnp.dot(left_basis.T, right_rotated, preferred_element_type=jnp.float32)
    new_first = 0.9 * first_moment + 0.1 * rotated
    new_second = 0.95 * second_moment + 0.05 * rotated * rotated
    first_fix = 1.0 - 0.9 ** 20
    second_fix = 1.0 - 0.95 ** 20
    step_rotated = (new_first / first_fix / (jnp.sqrt(new_second / second_fix) + 1e-08)).astype(jnp.bfloat16)
    back_left = jnp.dot(left_basis, step_rotated, preferred_element_type=jnp.float32).astype(jnp.bfloat16)
    update = jnp.dot(back_left, right_basis.T, preferred_element_type=jnp.float32)
    return (new_first, new_second, update)
```

```python
import functools

import jax
import jax.numpy as jnp
import numpy as np
from jax import lax
from jax.experimental import pallas as pl
from jax.experimental.pallas import tpu as pltpu
from jax.sharding import PartitionSpec as P

F32, BF16 = jnp.float32, jnp.bfloat16
VMEM_BYTES = 40 * 2**20
ANY = pl.BlockSpec(memory_space=pl.ANY)


def like(shape, dtype):
    return jax.ShapeDtypeStruct(tuple(shape), dtype)


class Order:
    def __init__(self):
        self.last = None

    def call(self, kernel, place, inputs, in_specs, outs, out_specs, grid, aliases=None):
        n_in = len(inputs)
        extra = [] if self.last is None else [self.last]

        def wrapped(place_ref, *refs):
            kernel(place_ref, refs[:n_in], refs[n_in + len(extra) :])

        got = pl.pallas_call(
            wrapped,
            out_shape=outs,
            grid_spec=pltpu.PrefetchScalarGridSpec(
                num_scalar_prefetch=1,
                grid=grid,
                in_specs=list(in_specs) + [ANY] * len(extra),
                out_specs=out_specs,
            ),
            input_output_aliases={k + 1: v for k, v in (aliases or {}).items()},
            compiler_params=pltpu.CompilerParams(vmem_limit_bytes=VMEM_BYTES),
            cost_estimate=pl.CostEstimate(flops=10**12, bytes_accessed=1, transcendentals=0),
        )(place, *inputs, *extra)
        self.last = got[0]
        return got


def streams(spots, gather):
    out = []
    for t in range(spots - 1):
        for parity in range(2):
            edges = range(parity, spots - 1, 2)
            if gather:
                pairs = [(e, e + 1) for e in edges if e >= t]
                pairs += [(e + 1, e) for e in edges if e + 1 <= spots - 1 - t]
            else:
                pairs = [(e, e + 1) for e in edges if e <= t]
                pairs += [(e + 1, e) for e in edges if e >= spots - 2 - t]
            if pairs:
                out.append((t, parity, pairs))
    return out


def slots_of(spots, gather):
    groups, users, slot, table = [], [], {}, []
    for t, parity, pairs in streams(spots, gather):
        who = {}
        for a, b in pairs:
            if gather:
                who[b] = b - (t + 1) if a < b else b + (t + 1)
            else:
                who[a] = a + (spots - 1 - t) if a < b else a - (spots - 1 - t)
        for k in range(len(groups) + 1):
            if k == len(groups):
                groups.append([])
                users.append({})
            if not set(users[k]) & set(who):
                break
        groups[k].append((t, parity))
        users[k].update(who)
        slot[t, parity] = k
    table = [[users[k].get(z, 0) for k in range(len(groups))] for z in range(spots)]
    return groups, slot, np.array(table, np.int32)


STEPS = {
    "pack": -30.0,
    "right": -10.0,
    "sum 1 1": 20.0,
    "sum 2 1": 37.0,
    "sum 2 0": 41.0,
    "left": 62.0,
    "fold": 87.0,
    "moments": 100.0,
    "unfold": 116.0,
    "back": 138.0,
    "pass 1 0": 163.1,
    "pass 1 1": 163.0,
    "pass 2 0": 184.0,
    "away": 205.0,
    "near": 226.0,
}
APART = 45.0


def nominal(step, index):
    if step == "end":
        return 1e6
    if step in STEPS:
        return STEPS[step] + APART * index
    kind, t, _ = step.split()
    return STEPS["left" if kind == "sum" else "pass 2 0"] - 1.0 / (1 + int(t)) + APART * index


def run(tasks):
    waiting = {k: next(task) for k, task in enumerate(tasks)}
    while waiting:
        k = min(waiting, key=lambda k: (nominal(waiting[k], k), k))
        try:
            waiting[k] = next(tasks[k])
        except StopIteration:
            del waiting[k]


def body(row_size, col_size, widths, gradient, left_basis, right_basis, first_moment, second_moment):
    height, columns = first_moment.shape
    spots = col_size // 2
    col, row = lax.axis_index("col"), lax.axis_index("row")
    at, core = col // 2, col % 2
    direct, square = row_size in (2, 4), row_size == 4
    slots = np.arange(row_size, dtype=np.int32)

    _, sum_slot, sum_table = slots_of(spots, False)
    groups, gather_slot, gather_table = slots_of(spots, True)
    n_sum, n_gather = sum_table.shape[1] + 1, gather_table.shape[1] + 1
    own = np.arange(spots, dtype=np.int32)[:, None]
    sum_table = np.concatenate([sum_table, own], 1)
    gather_table = np.concatenate([own, gather_table], 1)
    same = np.array(
        [[list(sum_table[z]).index(d) for d in gather_table[z]] for z in range(spots)], np.int32
    )
    table = np.concatenate([sum_table, gather_table, same], 1)
    place = jnp.concatenate(
        [
            core.astype(jnp.int32).reshape(1),
            (slots ^ row.astype(jnp.int32)) if direct else jnp.asarray(slots),
            jnp.asarray(table)[at],
        ]
    )
    at_row, at_sum = 1, 1 + row_size
    at_gather, at_same = at_sum + n_sum, at_sum + n_sum + n_gather

    order = Order()

    def swap(x):
        return lax.ppermute(x, "col", [(j, j ^ 1) for j in range(col_size)])

    def along(x, pairs):
        return lax.ppermute(x, "col", [(2 * a + c, 2 * b + c) for a, b in pairs for c in range(2)])

    def to_partner(x, s):
        return lax.ppermute(x, "row", [(i, i ^ s) for i in range(row_size)])

    def across(blocks):
        if not direct:
            return [lax.psum_scatter(jnp.concatenate(blocks), "row", scatter_dimension=0, tiled=True)]
        return [blocks[0]] + [
            to_partner(blocks[s], s) for s in range(1, row_size)
        ]

    def spread(block):
        if not direct:
            whole = lax.all_gather(block, "row", axis=0, tiled=False)
            return [whole[s] for s in range(row_size)]
        return across([block] * row_size)

    other_gradient = swap(gradient)

    def turn():
        def kernel(_, ins, outs):
            outs[0][...] = ins[0][...].T

        return order.call(
            kernel,
            place,
            [left_basis],
            [pl.BlockSpec((height, height), lambda s, p: (0, p[at_row + s]))],
            [like((row_size * height, height), BF16)],
            [pl.BlockSpec((height, height), lambda s, p: (s, 0))],
            (row_size,),
        )[0]

    def pack(first, width):
        stride = columns // width

        def kernel(_, ins, outs):
            outs[0][0] = ins[0][...]

        depth = right_basis.shape[0]
        return order.call(
            kernel,
            place,
            [right_basis],
            [
                pl.BlockSpec(
                    (depth, width),
                    lambda s, p: (0, (2 * p[at_sum + s] + 1 - p[0]) * stride + first // width),
                )
            ],
            [like((n_sum, depth, width), BF16)],
            [pl.BlockSpec((1, depth, width), lambda s, p: (s, 0, 0))],
            (n_sum,),
        )[0]

    def right(packed, first, width):
        stride = columns // width
        depth = right_basis.shape[0]

        def kernel(_, ins, outs):
            mine, theirs, basis, other = ins
            value = jnp.dot(mine[...], basis[...], preferred_element_type=F32)
            value += jnp.dot(theirs[...], other[0], preferred_element_type=F32)
            value = value.astype(BF16)
            for s in range(n_sum):

                @pl.when(pl.program_id(0) == s)
                def _(s=s):
                    outs[s][...] = value

        whole = pl.BlockSpec((height, depth), lambda s, p: (0, 0))
        return order.call(
            kernel,
            place,
            [gradient, other_gradient, right_basis, packed],
            [
                whole,
                whole,
                pl.BlockSpec(
                    (depth, width),
                    lambda s, p: (0, (2 * p[at_sum + s] + p[0]) * stride + first // width),
                ),
                pl.BlockSpec((1, depth, width), lambda s, p: (s, 0, 0)),
            ],
            [like((height, width), BF16)] * n_sum,
            [pl.BlockSpec((height, width), lambda s, p: (0, 0))] * n_sum,
            (n_sum,),
        )

    def add(x, y):
        def kernel(_, ins, outs):
            outs[0][...] = (ins[0][...].astype(F32) + ins[1][...].astype(F32)).astype(BF16)

        spec = pl.BlockSpec(x.shape, lambda s, p: (0, 0))
        return order.call(kernel, place, [x, y], [spec, spec], [like(x.shape, BF16)], [spec], (1,))[0]

    def hand_on(x, also=()):
        def kernel(_, ins, outs):
            pass

        return order.call(
            kernel, place, [x, *also], [ANY] * (1 + len(also)), [like(x.shape, BF16)], [ANY], (1,), {0: 0}
        )[0]

    def left_sums(terms):
        width = terms[0].shape[1]
        n = len(terms)
        half = height // 2

        def kernel(_, ins, outs):
            total = ins[0][...].astype(F32)
            for term in ins[1:n]:
                total += term[...].astype(F32)
            value = jnp.dot(ins[n][...], total.astype(BF16), preferred_element_type=F32).astype(BF16)
            for s in range(row_size):

                @pl.when(pl.program_id(0) == s)
                def _(s=s):
                    if not square:
                        outs[s][...] = value
                        return
                    keep, by_x, by_y, then_y, then_x = outs
                    if s == 0:
                        keep[...] = value
                    if s & 1:
                        by_x[s // 2] = value[:half]
                    if s & 2:
                        by_y[s - 2] = value[half:]
                    if s == 2:
                        then_y[...] = value[:half]
                    if s == 1:
                        then_x[...] = value[half:]

        spec = pl.BlockSpec((height, width), lambda s, p: (0, 0))
        if square:
            shapes = [(height, width), (2, half, width), (2, half, width), (half, width), (half, width)]
        else:
            shapes = [(height, width)] * row_size
        return order.call(
            kernel,
            place,
            [*terms, turned_left[0]],
            [spec] * n + [pl.BlockSpec((height, height), lambda s, p: (s, 0))],
            [like(shape, BF16) for shape in shapes],
            [pl.BlockSpec(shape, lambda s, p, zeros=(0,) * len(shape): zeros) for shape in shapes],
            (row_size,),
        )

    def whole_spec(x):
        return pl.BlockSpec(x.shape, lambda s, p, zeros=(0,) * x.ndim: zeros)

    def fold(then_y, got_x, then_x, got_y):
        def kernel(_, ins, outs):
            for k in range(2):
                outs[k][...] = (ins[2 * k][...].astype(F32) + ins[2 * k + 1][1].astype(F32)).astype(BF16)

        inputs = [then_y, got_x, then_x, got_y]
        outs = [like(then_y.shape, BF16)] * 2
        return order.call(
            kernel, place, inputs, [whole_spec(x) for x in inputs], outs, [whole_spec(x) for x in outs], (1,)
        )

    def unfold(upper, got_upper, lower, got_lower):
        def kernel(_, ins, outs):
            for k in range(2):
                outs[k][0] = ins[2 * k][...]
                outs[k][1] = ins[2 * k + 1][...]

        inputs = [upper, got_upper, lower, got_lower]
        outs = [like((2, *upper.shape), BF16)] * 2
        return order.call(
            kernel, place, inputs, [whole_spec(x) for x in inputs], outs, [whole_spec(x) for x in outs], (1,)
        )

    def left_times(blocks):
        width = blocks[0][0][0].shape[-1]
        tile = height // 3 if height % 48 == 0 else height
        inputs, layout = [], []
        for views in blocks:
            refs = []
            for x, k in views:
                n = next((n for n, y in enumerate(inputs) if x is y), len(inputs))
                if n == len(inputs):
                    inputs.append(x)
                refs.append((n, k))
            layout.append(refs)
        first = len(inputs)

        def kernel(_, ins, outs):
            total = 0.0
            for s, refs in enumerate(layout):
                parts = [ins[n][...] if k is None else ins[n][k] for n, k in refs]
                x = parts[0] if len(parts) == 1 else jnp.concatenate(parts, axis=0)
                total += jnp.dot(ins[first + s][...], x, preferred_element_type=F32)
            outs[0][...] = total.astype(BF16)

        return order.call(
            kernel,
            place,
            [*inputs, *([left_basis] * row_size)],
            [whole_spec(x) for x in inputs]
            + [
                pl.BlockSpec((tile, height), lambda r, p, s=s: (r, p[at_row + s]))
                for s in range(row_size)
            ],
            [like((height, width), BF16)],
            [pl.BlockSpec((tile, width), lambda r, p: (r, 0))],
            (height // tile,),
        )[0]

    kept = []

    def moments(parts, first, width):
        tile = height // 4 if height % 64 == 0 else height // 2
        per_half = height // 2 // tile
        first_fix = 1.0 - 0.9**20
        second_fix = 1.0 - 0.95**20
        inputs, specs, halves = [], [], [[], []]
        for part in parts:
            if not isinstance(part, list):
                for k in range(2):
                    halves[k].append(len(inputs))
                inputs.append(part)
                specs.append(pl.BlockSpec((tile, width), lambda r, p: (r, 0)))
                continue
            for k, (x, at_x) in enumerate(part):
                halves[k].append(len(inputs))
                inputs.append(x)
                low = k * per_half

                def at(r, p, low=low, at_x=at_x):
                    r = jnp.clip(r - low, 0, per_half - 1)
                    return (r, 0) if at_x is None else (at_x, r, 0)

                specs.append(pl.BlockSpec((tile, width) if at_x is None else (None, tile, width), at))
        n = len(inputs)

        def kernel(_, ins, outs):
            for k in range(2):

                @pl.when(pl.program_id(0) // per_half == k)
                def _(k=k):
                    rotated = sum(ins[m][...].astype(F32) for m in halves[k])
                    nf = 0.9 * ins[n][...] + 0.1 * rotated
                    ns = 0.95 * ins[n + 1][...] + 0.05 * rotated * rotated
                    outs[2][...] = nf
                    outs[3][...] = ns
                    outs[k][...] = (nf / first_fix / (jnp.sqrt(ns / second_fix) + 1e-08)).astype(BF16)

        spot = pl.BlockSpec((tile, width), lambda r, p: (r, first // width))
        half_specs = [
            pl.BlockSpec((tile, width), lambda r, p, k=k: (jnp.clip(r - k * per_half, 0, per_half - 1), 0))
            for k in range(2)
        ]
        upper, lower, *kept[:] = order.call(
            kernel,
            place,
            [*inputs, first_moment, second_moment, *kept],
            specs + [spot, spot] + [ANY] * len(kept),
            [like((height // 2, width), BF16)] * 2 + [like((height, columns), F32)] * 2,
            [*half_specs, spot, spot],
            (height // tile,),
            {n + 2: 2, n + 3: 3} if kept else None,
        )
        return upper, lower

    def back(chunks, mine, dtype, ends=(), both=False):
        depth = right_basis.shape[0]
        tile = min(256, depth)
        inputs, specs, layout = [], [], []
        whole = [pl.BlockSpec((height, width), lambda r, p: (0, 0)) for _, width, _, _ in chunks]
        for at_chunk, (first, width, packed, gathered) in enumerate(chunks):
            stride = columns // width
            for flip in range(2 if both else 1):
                for g in range(n_gather):
                    xs = [swap(x) for x in gathered[g]] if flip else gathered[g]
                    inputs += xs
                    specs += [whole[at_chunk]] * len(xs)
                    layout.append(len(xs))
                    if mine:

                        def at(r, p, g=g, flip=flip, stride=stride, first=first, width=width):
                            half = p[0] if flip == 0 else 1 - p[0]
                            return (r, (2 * p[at_gather + g] + half) * stride + first // width)

                        inputs.append(right_basis)
                        specs.append(pl.BlockSpec((tile, width), at))
                    else:
                        inputs.append(packed)
                        specs.append(
                            pl.BlockSpec((1, tile, width), lambda r, p, g=g: (p[at_same + g], r, 0))
                        )
        out_spec = pl.BlockSpec((height, tile), lambda r, p: (0, r))
        n = len(inputs)
        inputs += list(ends)
        specs += [out_spec] * len(ends)

        def kernel(_, ins, outs):
            total = jnp.zeros((height, tile), F32)
            k = 0
            for count in layout:
                x = ins[k][...]
                for more in ins[k + 1 : k + count]:
                    x = x + more[...]
                basis = ins[k + count][...] if mine else ins[k + count][0]
                total += lax.dot_general(x, basis, (((1,), (1,)), ((), ())), preferred_element_type=F32)
                k += count + 1
            for end in ins[n:]:
                total += end[...].astype(F32)
            outs[0][...] = total.astype(dtype)

        return order.call(
            kernel, place, inputs, specs, [like((height, depth), dtype)], [out_spec], (depth // tile,)
        )[0]

    held, totals, turned_left = [], [], []

    def chunk(index, first, width):
        yield "pack"
        packed = swap(pack(first, width))
        yield "right"
        blocks = right(packed, first, width)
        if index == 0:
            turned_left.append(turn())
        got = {}
        for t, parity, pairs in streams(spots, False):
            value = blocks[sum_slot[t, parity]]
            before = got.get((t - 1, 1 - parity))
            if before is not None:
                yield f"sum {t} {parity}"
                value = add(value, before)
            got[t, parity] = along(value, pairs)
        yield "left"
        sums = left_sums([blocks[n_sum - 1]] + [got[k] for k in got if k[0] == spots - 2])
        if square:
            keep, by_x, by_y, then_y, then_x = sums
            got_x, got_y = to_partner(by_x, 1), to_partner(by_y, 2)
            yield "fold"
            then_y, then_x = fold(then_y, got_x, then_x, got_y)
            last_y, last_x = to_partner(then_y, 2), to_partner(then_x, 1)
            parts = [keep, [(got_x, 0), (got_y, 0)], [(last_y, None), (last_x, None)]]
        else:
            parts = across(sums)
        yield "moments"
        upper, lower = moments(parts, first, width)
        if square:
            upper_y, lower_x = to_partner(upper, 2), to_partner(lower, 1)
            yield "unfold"
            uppers, lowers = unfold(upper, upper_y, lower, lower_x)
            by_x, by_y = to_partner(uppers, 1), to_partner(lowers, 2)
            steps = [
                [(upper, None), (lower, None)],
                [(by_x, 0), (lower_x, None)],
                [(upper_y, None), (by_y, 0)],
                [(by_x, 1), (by_y, 1)],
            ]
        else:
            steps = [[(x, None)] for x in spread(jnp.concatenate([upper, lower]))]
        yield "back"
        turned = left_times(steps)
        got = {}
        for t, parity, pairs in streams(spots, True):
            value = turned
            if t:
                before = (t - 1, 1 - parity)
                yield f"pass {t} {parity}"
                value = hand_on(got[before], [got[t - 1, parity]] if t > 1 and (t - 1, parity) in got else [])
                got[before] = value
            got[t, parity] = along(value, pairs)
        held.append((first, width, packed, [[turned]] + [[got[k] for k in group] for group in groups]))
        last = index == len(widths) - 1
        if index < len(widths) - 2:
            return
        if not last:
            yield "away"
            away = swap(back(held[: index + 1], False, BF16))
            yield "near"
            totals.extend([away, back(held[: index + 1], True, F32)])
        else:
            yield "end"
            totals[:] = [back(held[-1:], True, F32, totals, True)]

    run([chunk(k, first, width) for k, (first, width) in enumerate(widths)])
    return (kept[0], kept[1], totals[0])


def solution(mesh):
    row_size, col_size = mesh.shape["row"], mesh.shape["col"]

    def whole(gradient, *rest):
        columns = gradient.shape[1] // col_size
        width = columns // 2
        widths = [(first, width) for first in range(0, columns, width)]
        return jax.shard_map(
            functools.partial(body, row_size, col_size, widths),
            mesh=mesh,
            in_specs=(
                P("row", "col"),
                P("row", None),
                P("col", None),
                P("row", "col"),
                P("row", "col"),
            ),
            out_specs=(P("row", "col"), P("row", "col"), P("row", "col")),
            check_vma=False,
        )(gradient, *rest)

    return whole
```

```python
import functools

import jax
import jax.numpy as jnp
import numpy as np
from jax import lax
from jax.experimental import pallas as pl
from jax.experimental.pallas import tpu as pltpu
from jax.sharding import PartitionSpec as P

F32, BF16 = jnp.float32, jnp.bfloat16
VMEM_BYTES = 40 * 2**20
FLOPS_A_US = 10**10
ANY = pl.BlockSpec(memory_space=pl.ANY)


def like(shape, dtype):
    return jax.ShapeDtypeStruct(tuple(shape), dtype)


class Order:
    def __init__(self):
        self.last = None

    def call(self, us, kernel, place, inputs, in_specs, outs, out_specs, grid, aliases=None):
        n_in = len(inputs)
        extra = [] if self.last is None else [self.last]

        def wrapped(place_ref, *refs):
            kernel(place_ref, refs[:n_in], refs[n_in + len(extra) :])

        got = pl.pallas_call(
            wrapped,
            out_shape=outs,
            grid_spec=pltpu.PrefetchScalarGridSpec(
                num_scalar_prefetch=1,
                grid=grid,
                in_specs=list(in_specs) + [ANY] * len(extra),
                out_specs=out_specs,
            ),
            input_output_aliases={k + 1: v for k, v in (aliases or {}).items()},
            compiler_params=pltpu.CompilerParams(vmem_limit_bytes=VMEM_BYTES),
            cost_estimate=pl.CostEstimate(flops=int(us * FLOPS_A_US), bytes_accessed=1, transcendentals=0),
        )(place, *inputs, *extra)
        self.last = got[0]
        return got


def streams(spots, gather):
    out = []
    for t in range(spots - 1):
        for parity in range(2):
            edges = range(parity, spots - 1, 2)
            if gather:
                pairs = [(e, e + 1) for e in edges if e >= t]
                pairs += [(e + 1, e) for e in edges if e + 1 <= spots - 1 - t]
            else:
                pairs = [(e, e + 1) for e in edges if e <= t]
                pairs += [(e + 1, e) for e in edges if e >= spots - 2 - t]
            if pairs:
                out.append((t, parity, pairs))
    return out


def slots_of(spots, gather):
    groups, users, slot, table = [], [], {}, []
    for t, parity, pairs in streams(spots, gather):
        who = {}
        for a, b in pairs:
            if gather:
                who[b] = b - (t + 1) if a < b else b + (t + 1)
            else:
                who[a] = a + (spots - 1 - t) if a < b else a - (spots - 1 - t)
        for k in range(len(groups) + 1):
            if k == len(groups):
                groups.append([])
                users.append({})
            if not set(users[k]) & set(who):
                break
        groups[k].append((t, parity))
        users[k].update(who)
        slot[t, parity] = k
    table = [[users[k].get(z, 0) for k in range(len(groups))] for z in range(spots)]
    return groups, slot, np.array(table, np.int32)


STEPS = {
    "pack first": -24.0,
    "pack": -20.0,
    "right first": -16.0,
    "right": -4.0,
    "sum 1 1": 20.0,
    "sum 2 1": 37.0,
    "sum 2 0": 41.0,
    "left": 62.0,
    "fold": 88.0,
    "moments": 101.0,
    "unfold": 117.0,
    "back": 138.0,
    "pass 1 0": 163.1,
    "pass 1 1": 163.0,
    "pass 2 0": 184.0,
    "away": 205.0,
    "near": 186.0,
}
APART = 58.0


def nominal(step, index):
    if step == "end":
        return 1e6
    if step in STEPS:
        return STEPS[step] + APART * index
    kind, t, _ = step.split()
    return STEPS["left" if kind == "sum" else "pass 2 0"] - 1.0 / (1 + int(t)) + APART * index


TURNS = "000010100110101100101100101011111"


def run(short, tasks):
    waiting = {k: next(task) for k, task in enumerate(tasks)}
    turns = [int(k) for k in TURNS] if short else []
    while waiting:
        k = min(waiting, key=lambda k: (nominal(waiting[k], k), k))
        if turns:
            k = turns.pop(0)
        try:
            waiting[k] = next(tasks[k])
        except StopIteration:
            del waiting[k]


def body(row_size, col_size, widths, gradient, left_basis, right_basis, first_moment, second_moment):
    height, columns = first_moment.shape
    spots = col_size // 2
    col, row = lax.axis_index("col"), lax.axis_index("row")
    at, core = col // 2, col % 2
    direct, square = row_size in (2, 4), row_size == 4
    slots = np.arange(row_size, dtype=np.int32)

    _, sum_slot, sum_table = slots_of(spots, False)
    groups, gather_slot, gather_table = slots_of(spots, True)
    n_sum, n_gather = sum_table.shape[1] + 1, gather_table.shape[1] + 1
    own = np.arange(spots, dtype=np.int32)[:, None]
    sum_table = np.concatenate([sum_table, own], 1)
    gather_table = np.concatenate([own, gather_table], 1)
    same = np.array(
        [[list(sum_table[z]).index(d) for d in gather_table[z]] for z in range(spots)], np.int32
    )
    table = np.concatenate([sum_table, gather_table, same], 1)
    place = jnp.concatenate(
        [
            core.astype(jnp.int32).reshape(1),
            (slots ^ row.astype(jnp.int32)) if direct else jnp.asarray(slots),
            jnp.asarray(table)[at],
        ]
    )
    at_row, at_sum = 1, 1 + row_size
    at_gather, at_same = at_sum + n_sum, at_sum + n_sum + n_gather

    order = Order()

    def swap(x):
        return lax.ppermute(x, "col", [(j, j ^ 1) for j in range(col_size)])

    def along(x, pairs):
        return lax.ppermute(x, "col", [(2 * a + c, 2 * b + c) for a, b in pairs for c in range(2)])

    def to_partner(x, s):
        return lax.ppermute(x, "row", [(i, i ^ s) for i in range(row_size)])

    def across(blocks):
        if not direct:
            return [lax.psum_scatter(jnp.concatenate(blocks), "row", scatter_dimension=0, tiled=True)]
        return [blocks[0]] + [
            to_partner(blocks[s], s) for s in range(1, row_size)
        ]

    def spread(block):
        if not direct:
            whole = lax.all_gather(block, "row", axis=0, tiled=False)
            return [whole[s] for s in range(row_size)]
        return across([block] * row_size)

    other_gradient = swap(gradient)

    def turn():
        def kernel(_, ins, outs):
            outs[0][...] = ins[0][...].T

        return order.call(
            4.0,
            kernel,
            place,
            [left_basis],
            [pl.BlockSpec((height, height), lambda s, p: (0, p[at_row + s]))],
            [like((row_size * height, height), BF16)],
            [pl.BlockSpec((height, height), lambda s, p: (s, 0))],
            (row_size,),
        )[0]

    def pack(first, width, low, high):
        stride = columns // width

        def kernel(_, ins, outs):
            outs[0][0] = ins[0][...]

        depth = right_basis.shape[0]
        return order.call(
            1.5 * (high - low),
            kernel,
            place,
            [right_basis],
            [
                pl.BlockSpec(
                    (depth, width),
                    lambda s, p: (0, (2 * p[at_sum + low + s] + 1 - p[0]) * stride + first // width),
                )
            ],
            [like((high - low, depth, width), BF16)],
            [pl.BlockSpec((1, depth, width), lambda s, p: (s, 0, 0))],
            (high - low,),
        )[0]

    def right(packed, first, width, low, high):
        stride = columns // width
        depth = right_basis.shape[0]

        def kernel(_, ins, outs):
            mine, theirs, basis, other = ins
            value = jnp.dot(mine[...], basis[...], preferred_element_type=F32)
            value += jnp.dot(theirs[...], other[0], preferred_element_type=F32)
            value = value.astype(BF16)
            for s in range(high - low):

                @pl.when(pl.program_id(0) == s)
                def _(s=s):
                    outs[s][...] = value

        whole = pl.BlockSpec((height, depth), lambda s, p: (0, 0))
        return order.call(
            2.5 * (high - low),
            kernel,
            place,
            [gradient, other_gradient, right_basis, packed],
            [
                whole,
                whole,
                pl.BlockSpec(
                    (depth, width),
                    lambda s, p: (0, (2 * p[at_sum + low + s] + p[0]) * stride + first // width),
                ),
                pl.BlockSpec((1, depth, width), lambda s, p: (s, 0, 0)),
            ],
            [like((height, width), BF16)] * (high - low),
            [pl.BlockSpec((height, width), lambda s, p: (0, 0))] * (high - low),
            (high - low,),
        )

    def add(x, y):
        def kernel(_, ins, outs):
            outs[0][...] = (ins[0][...].astype(F32) + ins[1][...].astype(F32)).astype(BF16)

        spec = pl.BlockSpec(x.shape, lambda s, p: (0, 0))
        return order.call(2.0, kernel, place, [x, y], [spec, spec], [like(x.shape, BF16)], [spec], (1,))[0]

    def hand_on(x, also=()):
        def kernel(_, ins, outs):
            pass

        return order.call(
            0.5,
            kernel, place, [x, *also], [ANY] * (1 + len(also)), [like(x.shape, BF16)], [ANY], (1,), {0: 0}
        )[0]

    def left_sums(terms):
        width = terms[0].shape[1]
        n = len(terms)
        half = height // 2

        def kernel(_, ins, outs):
            total = ins[0][...].astype(F32)
            for term in ins[1:n]:
                total += term[...].astype(F32)
            value = jnp.dot(ins[n][...], total.astype(BF16), preferred_element_type=F32).astype(BF16)
            for s in range(row_size):

                @pl.when(pl.program_id(0) == s)
                def _(s=s):
                    if not square:
                        outs[s][...] = value
                        return
                    keep, by_x, by_y, then_y, then_x = outs
                    if s == 0:
                        keep[...] = value
                    if s & 1:
                        by_x[s // 2] = value[:half]
                    if s & 2:
                        by_y[s - 2] = value[half:]
                    if s == 2:
                        then_y[...] = value[:half]
                    if s == 1:
                        then_x[...] = value[half:]

        spec = pl.BlockSpec((height, width), lambda s, p: (0, 0))
        if square:
            shapes = [(height, width), (2, half, width), (2, half, width), (half, width), (half, width)]
        else:
            shapes = [(height, width)] * row_size
        return order.call(
            5.0,
            kernel,
            place,
            [*terms, turned_left[0]],
            [spec] * n + [pl.BlockSpec((height, height), lambda s, p: (s, 0))],
            [like(shape, BF16) for shape in shapes],
            [pl.BlockSpec(shape, lambda s, p, zeros=(0,) * len(shape): zeros) for shape in shapes],
            (row_size,),
        )

    def whole_spec(x):
        return pl.BlockSpec(x.shape, lambda s, p, zeros=(0,) * x.ndim: zeros)

    def fold(then_y, got_x, then_x, got_y):
        def kernel(_, ins, outs):
            for k in range(2):
                outs[k][...] = (ins[2 * k][...].astype(F32) + ins[2 * k + 1][1].astype(F32)).astype(BF16)

        inputs = [then_y, got_x, then_x, got_y]
        outs = [like(then_y.shape, BF16)] * 2
        return order.call(
            1.0,
            kernel, place, inputs, [whole_spec(x) for x in inputs], outs, [whole_spec(x) for x in outs], (1,)
        )

    def unfold(upper, got_upper, lower, got_lower):
        def kernel(_, ins, outs):
            for k in range(2):
                outs[k][0] = ins[2 * k][...]
                outs[k][1] = ins[2 * k + 1][...]

        inputs = [upper, got_upper, lower, got_lower]
        outs = [like((2, *upper.shape), BF16)] * 2
        return order.call(
            1.5,
            kernel, place, inputs, [whole_spec(x) for x in inputs], outs, [whole_spec(x) for x in outs], (1,)
        )

    def left_times(blocks):
        width = blocks[0][0][0].shape[-1]
        tile = height // 3 if height % 48 == 0 else height
        inputs, layout = [], []
        for views in blocks:
            refs = []
            for x, k in views:
                n = next((n for n, y in enumerate(inputs) if x is y), len(inputs))
                if n == len(inputs):
                    inputs.append(x)
                refs.append((n, k))
            layout.append(refs)
        first = len(inputs)

        def kernel(_, ins, outs):
            total = 0.0
            for s, refs in enumerate(layout):
                parts = [ins[n][...] if k is None else ins[n][k] for n, k in refs]
                x = parts[0] if len(parts) == 1 else jnp.concatenate(parts, axis=0)
                total += jnp.dot(ins[first + s][...], x, preferred_element_type=F32)
            outs[0][...] = total.astype(BF16)

        return order.call(
            5.0,
            kernel,
            place,
            [*inputs, *([left_basis] * row_size)],
            [whole_spec(x) for x in inputs]
            + [
                pl.BlockSpec((tile, height), lambda r, p, s=s: (r, p[at_row + s]))
                for s in range(row_size)
            ],
            [like((height, width), BF16)],
            [pl.BlockSpec((tile, width), lambda r, p: (r, 0))],
            (height // tile,),
        )[0]

    kept = []

    def moments(parts, first, width):
        tile = height // 4 if height % 64 == 0 else height // 2
        per_half = height // 2 // tile
        first_fix = 1.0 - 0.9**20
        second_fix = 1.0 - 0.95**20
        inputs, specs, halves = [], [], [[], []]
        for part in parts:
            if not isinstance(part, list):
                for k in range(2):
                    halves[k].append(len(inputs))
                inputs.append(part)
                specs.append(pl.BlockSpec((tile, width), lambda r, p: (r, 0)))
                continue
            for k, (x, at_x) in enumerate(part):
                halves[k].append(len(inputs))
                inputs.append(x)
                low = k * per_half

                def at(r, p, low=low, at_x=at_x):
                    r = jnp.clip(r - low, 0, per_half - 1)
                    return (r, 0) if at_x is None else (at_x, r, 0)

                specs.append(pl.BlockSpec((tile, width) if at_x is None else (None, tile, width), at))
        n = len(inputs)

        def kernel(_, ins, outs):
            for k in range(2):

                @pl.when(pl.program_id(0) // per_half == k)
                def _(k=k):
                    rotated = sum(ins[m][...].astype(F32) for m in halves[k])
                    nf = 0.9 * ins[n][...] + 0.1 * rotated
                    ns = 0.95 * ins[n + 1][...] + 0.05 * rotated * rotated
                    outs[2][...] = nf
                    outs[3][...] = ns
                    outs[k][...] = (nf / first_fix / (jnp.sqrt(ns / second_fix) + 1e-08)).astype(BF16)

        spot = pl.BlockSpec((tile, width), lambda r, p: (r, first // width))
        half_specs = [
            pl.BlockSpec((tile, width), lambda r, p, k=k: (jnp.clip(r - k * per_half, 0, per_half - 1), 0))
            for k in range(2)
        ]
        upper, lower, *kept[:] = order.call(
            5.0,
            kernel,
            place,
            [*inputs, first_moment, second_moment, *kept],
            specs + [spot, spot] + [ANY] * len(kept),
            [like((height // 2, width), BF16)] * 2 + [like((height, columns), F32)] * 2,
            [*half_specs, spot, spot],
            (height // tile,),
            {n + 2: 2, n + 3: 3} if kept else None,
        )
        return upper, lower

    def back(chunks, mine, dtype, ends=(), both=False, some=None):
        depth = right_basis.shape[0]
        tile = min(256, depth)
        inputs, specs, layout, at_g = [], [], [], []
        whole = [pl.BlockSpec((height, width), lambda r, p: (0, 0)) for _, width, _, _ in chunks]
        for at_chunk, (first, width, packed, gathered) in enumerate(chunks):
            stride = columns // width
            for flip in range(2 if both else 1):
                for g in range(n_gather) if some is None else some:
                    xs = [swap(x) for x in gathered[g]] if flip else gathered[g]
                    inputs += xs
                    specs += [whole[at_chunk]] * len(xs)
                    layout.append(len(xs))
                    at_g.append(g)
                    if mine:

                        def at(r, p, g=g, flip=flip, stride=stride, first=first, width=width):
                            half = p[0] if flip == 0 else 1 - p[0]
                            return (r, (2 * p[at_gather + g] + half) * stride + first // width)

                        inputs.append(right_basis)
                        specs.append(pl.BlockSpec((tile, width), at))
                    else:
                        for k, x in enumerate(packed):
                            low, high = (0, 1) if k == 0 else (1, n_sum)

                            def at_packed(r, p, g=g, low=low, high=high):
                                return (jnp.clip(p[at_same + g] - low, 0, high - low - 1), r, 0)

                            inputs.append(x)
                            specs.append(pl.BlockSpec((1, tile, width), at_packed))
        out_spec = pl.BlockSpec((height, tile), lambda r, p: (0, r))
        n = len(inputs)
        inputs += list(ends)
        specs += [out_spec] * len(ends)

        def kernel(p_ref, ins, outs):
            total = jnp.zeros((height, tile), F32)
            k = 0
            for j, count in enumerate(layout):
                x = ins[k][...]
                for more in ins[k + 1 : k + count]:
                    x = x + more[...]
                if mine:
                    basis = ins[k + count][...]
                else:
                    basis = jnp.where(p_ref[at_same + at_g[j]] == 0, ins[k + count][0], ins[k + count + 1][0])
                total += lax.dot_general(x, basis, (((1,), (1,)), ((), ())), preferred_element_type=F32)
                k += count + (1 if mine else 2)
            for end in ins[n:]:
                total += end[...].astype(F32)
            outs[0][...] = total.astype(dtype)

        return order.call(
            8.0,
            kernel, place, inputs, specs, [like((height, depth), dtype)], [out_spec], (depth // tile,)
        )[0]

    held, totals, turned_left = [], [], []

    def chunk(index, first, width):
        parts = ((0, 1), (1, n_sum))
        yield "pack first"
        packed = [swap(pack(first, width, *parts[0]))]
        yield "pack"
        packed.append(swap(pack(first, width, *parts[1])))
        yield "right first"
        blocks = list(right(packed[0], first, width, *parts[0]))
        early = along(blocks[0], streams(spots, False)[0][2])
        if index == 0:
            turned_left.append(turn())
        yield "right"
        blocks += right(packed[1], first, width, *parts[1])
        got = {}
        for t, parity, pairs in sorted(streams(spots, False), key=lambda x: x[:2]):
            value = blocks[sum_slot[t, parity]]
            before = got.get((t - 1, 1 - parity))
            if before is not None:
                yield f"sum {t} {parity}"
                value = add(value, before)
            got[t, parity] = along(value, pairs) if got else early
        yield "left"
        sums = left_sums([blocks[n_sum - 1]] + [got[k] for k in got if k[0] == spots - 2])
        if square:
            keep, by_x, by_y, then_y, then_x = sums
            got_x, got_y = to_partner(by_x, 1), to_partner(by_y, 2)
            yield "fold"
            then_y, then_x = fold(then_y, got_x, then_x, got_y)
            last_y, last_x = to_partner(then_y, 2), to_partner(then_x, 1)
            parts = [keep, [(got_x, 0), (got_y, 0)], [(last_y, None), (last_x, None)]]
        else:
            parts = across(sums)
        yield "moments"
        upper, lower = moments(parts, first, width)
        if square:
            upper_y, lower_x = to_partner(upper, 2), to_partner(lower, 1)
            yield "unfold"
            uppers, lowers = unfold(upper, upper_y, lower, lower_x)
            by_x, by_y = to_partner(uppers, 1), to_partner(lowers, 2)
            steps = [
                [(upper, None), (lower, None)],
                [(by_x, 0), (lower_x, None)],
                [(upper_y, None), (by_y, 0)],
                [(by_x, 1), (by_y, 1)],
            ]
        else:
            steps = [[(x, None)] for x in spread(jnp.concatenate([upper, lower]))]
        yield "back"
        turned = left_times(steps)
        got = {}
        for t, parity, pairs in streams(spots, True):
            value = turned
            if t:
                before = (t - 1, 1 - parity)
                yield f"pass {t} {parity}"
                value = hand_on(got[before], [got[t - 1, parity]] if t > 1 and (t - 1, parity) in got else [])
                got[before] = value
            got[t, parity] = along(value, pairs)
        held.append((first, width, packed, [[turned]] + [[got[k] for k in group] for group in groups]))
        last = index == len(widths) - 1
        if index < len(widths) - 2:
            return
        if not last:
            yield "away"
            away = swap(back(held[: index + 1], False, BF16))
            totals.append(away)
        else:
            yield "near"
            half = n_gather - 1
            most = back(held[-1:], True, F32, (), True, range(half))
            if index:
                totals.append(back(held[:-1], True, F32, [most]))
            else:
                totals.append(most)
            yield "end"
            final = held[-1][3][-1]
            final[:] = [hand_on(x) for x in final]
            totals[:] = [back(held[-1:], True, F32, totals, True, range(half, n_gather))]

    run(spots == 4, [chunk(k, first, width) for k, (first, width) in enumerate(widths)])
    return (kept[0], kept[1], totals[0])


def solution(mesh):
    row_size, col_size = mesh.shape["row"], mesh.shape["col"]

    def whole(gradient, *rest):
        columns = gradient.shape[1] // col_size
        width = columns // 2
        widths = [(first, width) for first in range(0, columns, width)]
        return jax.shard_map(
            functools.partial(body, row_size, col_size, widths),
            mesh=mesh,
            in_specs=(
                P("row", "col"),
                P("row", None),
                P("col", None),
                P("row", "col"),
                P("row", "col"),
            ),
            out_specs=(P("row", "col"), P("row", "col"), P("row", "col")),
            check_vma=False,
        )(gradient, *rest)

    return whole
```

```python
import functools

import jax
import jax.numpy as jnp
import numpy as np
from jax import lax
from jax.experimental import pallas as pl
from jax.experimental.pallas import tpu as pltpu
from jax.sharding import PartitionSpec as P

F32, BF16 = jnp.float32, jnp.bfloat16
VMEM_BYTES = 38 * 2**20
FLOPS_A_US = 6000000000
ANY = pl.BlockSpec(memory_space=pl.ANY)


def like(shape, dtype):
    return jax.ShapeDtypeStruct(tuple(shape), dtype)


class Order:
    def __init__(self):
        self.last = None

    def call(self, us, kernel, place, inputs, in_specs, outs, out_specs, grid, aliases=None):
        n_in = len(inputs)
        extra = [] if self.last is None else [self.last]

        def wrapped(place_ref, *refs):
            kernel(place_ref, refs[:n_in], refs[n_in + len(extra) :])

        got = pl.pallas_call(
            wrapped,
            out_shape=outs,
            grid_spec=pltpu.PrefetchScalarGridSpec(
                num_scalar_prefetch=1,
                grid=grid,
                in_specs=list(in_specs) + [ANY] * len(extra),
                out_specs=out_specs,
            ),
            input_output_aliases={k + 1: v for k, v in (aliases or {}).items()},
            compiler_params=pltpu.CompilerParams(vmem_limit_bytes=VMEM_BYTES),
            cost_estimate=pl.CostEstimate(flops=int(us * FLOPS_A_US), bytes_accessed=1, transcendentals=0),
        )(place, *inputs, *extra)
        self.last = got[0]
        return got


def streams(spots, gather):
    out = []
    for t in range(spots - 1):
        for parity in range(2):
            edges = range(parity, spots - 1, 2)
            if gather:
                pairs = [(e, e + 1) for e in edges if e >= t]
                pairs += [(e + 1, e) for e in edges if e + 1 <= spots - 1 - t]
            else:
                pairs = [(e, e + 1) for e in edges if e <= t]
                pairs += [(e + 1, e) for e in edges if e >= spots - 2 - t]
            if pairs:
                out.append((t, parity, pairs))
    return out


def slots_of(spots, gather):
    groups, users, slot, table = [], [], {}, []
    for t, parity, pairs in streams(spots, gather):
        who = {}
        for a, b in pairs:
            if gather:
                who[b] = b - (t + 1) if a < b else b + (t + 1)
            else:
                who[a] = a + (spots - 1 - t) if a < b else a - (spots - 1 - t)
        for k in range(len(groups) + 1):
            if k == len(groups):
                groups.append([])
                users.append({})
            if not set(users[k]) & set(who):
                break
        groups[k].append((t, parity))
        users[k].update(who)
        slot[t, parity] = k
    table = [[users[k].get(z, 0) for k in range(len(groups))] for z in range(spots)]
    return groups, slot, np.array(table, np.int32)


STEPS = {
    "pack first": -24.0,
    "pack": -20.0,
    "right first": -16.0,
    "right": -4.0,
    "sum 1 1": 20.0,
    "sum 2 1": 37.0,
    "sum 2 0": 41.0,
    "left": 62.0,
    "fold": 88.0,
    "moments": 101.0,
    "unfold": 117.0,
    "back": 138.0,
    "pass 1 0": 163.1,
    "pass 1 1": 163.0,
    "pass 2 0": 184.0,
    "away": 205.0,
    "near": 186.0,
}
APART = 58.0


def nominal(step, index):
    if step == "end":
        return 1e6
    if step in STEPS:
        return STEPS[step] + APART * index
    kind, t, _ = step.split()
    return STEPS["left" if kind == "sum" else "pass 2 0"] - 1.0 / (1 + int(t)) + APART * index


TURNS = "000010100110101100101100101011111"


def run(short, tasks):
    waiting = {k: next(task) for k, task in enumerate(tasks)}
    turns = [int(k) for k in TURNS] if short else []
    while waiting:
        k = min(waiting, key=lambda k: (nominal(waiting[k], k), k))
        if turns:
            k = turns.pop(0)
        try:
            waiting[k] = next(tasks[k])
        except StopIteration:
            del waiting[k]


def body(row_size, col_size, widths, gradient, left_basis, right_basis, first_moment, second_moment):
    height, columns = first_moment.shape
    spots = col_size // 2
    col, row = lax.axis_index("col"), lax.axis_index("row")
    at, core = col // 2, col % 2
    direct, square = row_size in (2, 4), row_size == 4
    slots = np.arange(row_size, dtype=np.int32)

    _, sum_slot, sum_table = slots_of(spots, False)
    groups, gather_slot, gather_table = slots_of(spots, True)
    n_sum, n_gather = sum_table.shape[1] + 1, gather_table.shape[1] + 1
    own = np.arange(spots, dtype=np.int32)[:, None]
    sum_table = np.concatenate([sum_table, own], 1)
    gather_table = np.concatenate([own, gather_table], 1)
    same = np.array(
        [[list(sum_table[z]).index(d) for d in gather_table[z]] for z in range(spots)], np.int32
    )
    table = np.concatenate([sum_table, gather_table, same], 1)
    place = jnp.concatenate(
        [
            core.astype(jnp.int32).reshape(1),
            (slots ^ row.astype(jnp.int32)) if direct else jnp.asarray(slots),
            jnp.asarray(table)[at],
        ]
    )
    at_row, at_sum = 1, 1 + row_size
    at_gather, at_same = at_sum + n_sum, at_sum + n_sum + n_gather

    order = Order()

    def swap(x):
        return lax.ppermute(x, "col", [(j, j ^ 1) for j in range(col_size)])

    def along(x, pairs):
        return lax.ppermute(x, "col", [(2 * a + c, 2 * b + c) for a, b in pairs for c in range(2)])

    def to_partner(x, s):
        return lax.ppermute(x, "row", [(i, i ^ s) for i in range(row_size)])

    def across(blocks):
        if not direct:
            return [lax.psum_scatter(jnp.concatenate(blocks), "row", scatter_dimension=0, tiled=True)]
        return [blocks[0]] + [
            to_partner(blocks[s], s) for s in range(1, row_size)
        ]

    def spread(block):
        if not direct:
            whole = lax.all_gather(block, "row", axis=0, tiled=False)
            return [whole[s] for s in range(row_size)]
        return across([block] * row_size)

    other_gradient = swap(gradient)

    def turn():
        def kernel(_, ins, outs):
            outs[0][...] = ins[0][...].T

        return order.call(
            4.0,
            kernel,
            place,
            [left_basis],
            [pl.BlockSpec((height, height), lambda s, p: (0, p[at_row + s]))],
            [like((row_size * height, height), BF16)],
            [pl.BlockSpec((height, height), lambda s, p: (s, 0))],
            (row_size,),
        )[0]

    def pack(first, width, low, high):
        stride = columns // width

        def kernel(_, ins, outs):
            outs[0][0] = ins[0][...]

        depth = right_basis.shape[0]
        return order.call(
            1.5 * (high - low),
            kernel,
            place,
            [right_basis],
            [
                pl.BlockSpec(
                    (depth, width),
                    lambda s, p: (0, (2 * p[at_sum + low + s] + 1 - p[0]) * stride + first // width),
                )
            ],
            [like((high - low, depth, width), BF16)],
            [pl.BlockSpec((1, depth, width), lambda s, p: (s, 0, 0))],
            (high - low,),
        )[0]

    def right(packed, first, width, low, high):
        stride = columns // width
        depth = right_basis.shape[0]

        def kernel(_, ins, outs):
            mine, theirs, basis, other = ins
            value = jnp.dot(mine[...], basis[...], preferred_element_type=F32)
            value += jnp.dot(theirs[...], other[0], preferred_element_type=F32)
            value = value.astype(BF16)
            for s in range(high - low):

                @pl.when(pl.program_id(0) == s)
                def _(s=s):
                    outs[s][...] = value

        whole = pl.BlockSpec((height, depth), lambda s, p: (0, 0))
        return order.call(
            2.5 * (high - low),
            kernel,
            place,
            [gradient, other_gradient, right_basis, packed],
            [
                whole,
                whole,
                pl.BlockSpec(
                    (depth, width),
                    lambda s, p: (0, (2 * p[at_sum + low + s] + p[0]) * stride + first // width),
                ),
                pl.BlockSpec((1, depth, width), lambda s, p: (s, 0, 0)),
            ],
            [like((height, width), BF16)] * (high - low),
            [pl.BlockSpec((height, width), lambda s, p: (0, 0))] * (high - low),
            (high - low,),
        )

    def add(x, y):
        def kernel(_, ins, outs):
            outs[0][...] = (ins[0][...].astype(F32) + ins[1][...].astype(F32)).astype(BF16)

        spec = pl.BlockSpec(x.shape, lambda s, p: (0, 0))
        return order.call(2.0, kernel, place, [x, y], [spec, spec], [like(x.shape, BF16)], [spec], (1,))[0]

    def hand_on(x, also=()):
        def kernel(_, ins, outs):
            pass

        return order.call(
            0.5,
            kernel, place, [x, *also], [ANY] * (1 + len(also)), [like(x.shape, BF16)], [ANY], (1,), {0: 0}
        )[0]

    def left_sums(terms):
        width = terms[0].shape[1]
        n = len(terms)
        half = height // 2

        def kernel(_, ins, outs):
            total = ins[0][...].astype(F32)
            for term in ins[1:n]:
                total += term[...].astype(F32)
            value = jnp.dot(ins[n][...], total.astype(BF16), preferred_element_type=F32).astype(BF16)
            for s in range(row_size):

                @pl.when(pl.program_id(0) == s)
                def _(s=s):
                    if not square:
                        outs[s][...] = value
                        return
                    keep, by_x, by_y, then_y, then_x = outs
                    if s == 0:
                        keep[...] = value
                    if s & 1:
                        by_x[s // 2] = value[:half]
                    if s & 2:
                        by_y[s - 2] = value[half:]
                    if s == 2:
                        then_y[...] = value[:half]
                    if s == 1:
                        then_x[...] = value[half:]

        spec = pl.BlockSpec((height, width), lambda s, p: (0, 0))
        if square:
            shapes = [(height, width), (2, half, width), (2, half, width), (half, width), (half, width)]
        else:
            shapes = [(height, width)] * row_size
        return order.call(
            5.0,
            kernel,
            place,
            [*terms, turned_left[0]],
            [spec] * n + [pl.BlockSpec((height, height), lambda s, p: (s, 0))],
            [like(shape, BF16) for shape in shapes],
            [pl.BlockSpec(shape, lambda s, p, zeros=(0,) * len(shape): zeros) for shape in shapes],
            (row_size,),
        )

    def whole_spec(x):
        return pl.BlockSpec(x.shape, lambda s, p, zeros=(0,) * x.ndim: zeros)

    def fold(then_y, got_x, then_x, got_y):
        def kernel(_, ins, outs):
            for k in range(2):
                outs[k][...] = (ins[2 * k][...].astype(F32) + ins[2 * k + 1][1].astype(F32)).astype(BF16)

        inputs = [then_y, got_x, then_x, got_y]
        outs = [like(then_y.shape, BF16)] * 2
        return order.call(
            1.0,
            kernel, place, inputs, [whole_spec(x) for x in inputs], outs, [whole_spec(x) for x in outs], (1,)
        )

    def unfold(upper, got_upper, lower, got_lower):
        def kernel(_, ins, outs):
            for k in range(2):
                outs[k][0] = ins[2 * k][...]
                outs[k][1] = ins[2 * k + 1][...]

        inputs = [upper, got_upper, lower, got_lower]
        outs = [like((2, *upper.shape), BF16)] * 2
        return order.call(
            1.5,
            kernel, place, inputs, [whole_spec(x) for x in inputs], outs, [whole_spec(x) for x in outs], (1,)
        )

    def left_times(blocks):
        width = blocks[0][0][0].shape[-1]
        tile = height // 3 if height % 48 == 0 else height
        inputs, layout = [], []
        for views in blocks:
            refs = []
            for x, k in views:
                n = next((n for n, y in enumerate(inputs) if x is y), len(inputs))
                if n == len(inputs):
                    inputs.append(x)
                refs.append((n, k))
            layout.append(refs)
        first = len(inputs)

        def kernel(_, ins, outs):
            total = 0.0
            for s, refs in enumerate(layout):
                parts = [ins[n][...] if k is None else ins[n][k] for n, k in refs]
                x = parts[0] if len(parts) == 1 else jnp.concatenate(parts, axis=0)
                total += jnp.dot(ins[first + s][...], x, preferred_element_type=F32)
            outs[0][...] = total.astype(BF16)

        return order.call(
            5.0,
            kernel,
            place,
            [*inputs, *([left_basis] * row_size)],
            [whole_spec(x) for x in inputs]
            + [
                pl.BlockSpec((tile, height), lambda r, p, s=s: (r, p[at_row + s]))
                for s in range(row_size)
            ],
            [like((height, width), BF16)],
            [pl.BlockSpec((tile, width), lambda r, p: (r, 0))],
            (height // tile,),
        )[0]

    kept = []

    def moments(parts, first, width):
        tile = height // 4 if height % 64 == 0 else height // 2
        per_half = height // 2 // tile
        first_fix = 1.0 - 0.9**20
        second_fix = 1.0 - 0.95**20
        inputs, specs, halves = [], [], [[], []]
        for part in parts:
            if not isinstance(part, list):
                for k in range(2):
                    halves[k].append(len(inputs))
                inputs.append(part)
                specs.append(pl.BlockSpec((tile, width), lambda r, p: (r, 0)))
                continue
            for k, (x, at_x) in enumerate(part):
                halves[k].append(len(inputs))
                inputs.append(x)
                low = k * per_half

                def at(r, p, low=low, at_x=at_x):
                    r = jnp.clip(r - low, 0, per_half - 1)
                    return (r, 0) if at_x is None else (at_x, r, 0)

                specs.append(pl.BlockSpec((tile, width) if at_x is None else (None, tile, width), at))
        n = len(inputs)

        def kernel(_, ins, outs):
            for k in range(2):

                @pl.when(pl.program_id(0) // per_half == k)
                def _(k=k):
                    rotated = sum(ins[m][...].astype(F32) for m in halves[k])
                    nf = 0.9 * ins[n][...] + 0.1 * rotated
                    ns = 0.95 * ins[n + 1][...] + 0.05 * rotated * rotated
                    outs[2][...] = nf
                    outs[3][...] = ns
                    outs[k][...] = (nf / first_fix / (jnp.sqrt(ns / second_fix) + 1e-08)).astype(BF16)

        spot = pl.BlockSpec((tile, width), lambda r, p: (r, first // width))
        half_specs = [
            pl.BlockSpec((tile, width), lambda r, p, k=k: (jnp.clip(r - k * per_half, 0, per_half - 1), 0))
            for k in range(2)
        ]
        upper, lower, *kept[:] = order.call(
            5.0,
            kernel,
            place,
            [*inputs, first_moment, second_moment, *kept],
            specs + [spot, spot] + [ANY] * len(kept),
            [like((height // 2, width), BF16)] * 2 + [like((height, columns), F32)] * 2,
            [*half_specs, spot, spot],
            (height // tile,),
            {n + 2: 2, n + 3: 3} if kept else None,
        )
        return upper, lower

    def back(chunks, mine, dtype, ends=(), both=False, some=None):
        depth = right_basis.shape[0]
        tile = min(256, depth)
        inputs, specs, layout, at_g = [], [], [], []
        whole = [pl.BlockSpec((height, width), lambda r, p: (0, 0)) for _, width, _, _ in chunks]
        for at_chunk, (first, width, packed, gathered) in enumerate(chunks):
            stride = columns // width
            for flip in range(2 if both else 1):
                for g in range(n_gather) if some is None else some:
                    xs = [swap(x) for x in gathered[g]] if flip else gathered[g]
                    inputs += xs
                    specs += [whole[at_chunk]] * len(xs)
                    layout.append(len(xs))
                    at_g.append(g)
                    if mine:

                        def at(r, p, g=g, flip=flip, stride=stride, first=first, width=width):
                            half = p[0] if flip == 0 else 1 - p[0]
                            return (r, (2 * p[at_gather + g] + half) * stride + first // width)

                        inputs.append(right_basis)
                        specs.append(pl.BlockSpec((tile, width), at))
                    else:
                        for k, x in enumerate(packed):
                            low, high = (0, 1) if k == 0 else (1, n_sum)

                            def at_packed(r, p, g=g, low=low, high=high):
                                return (jnp.clip(p[at_same + g] - low, 0, high - low - 1), r, 0)

                            inputs.append(x)
                            specs.append(pl.BlockSpec((1, tile, width), at_packed))
        out_spec = pl.BlockSpec((height, tile), lambda r, p: (0, r))
        n = len(inputs)
        inputs += list(ends)
        specs += [out_spec] * len(ends)

        def kernel(p_ref, ins, outs):
            total = jnp.zeros((height, tile), F32)
            k = 0
            for j, count in enumerate(layout):
                x = ins[k][...]
                for more in ins[k + 1 : k + count]:
                    x = x + more[...]
                if mine:
                    basis = ins[k + count][...]
                else:
                    basis = jnp.where(p_ref[at_same + at_g[j]] == 0, ins[k + count][0], ins[k + count + 1][0])
                total += lax.dot_general(x, basis, (((1,), (1,)), ((), ())), preferred_element_type=F32)
                k += count + (1 if mine else 2)
            for end in ins[n:]:
                total += end[...].astype(F32)
            outs[0][...] = total.astype(dtype)

        return order.call(
            8.0,
            kernel, place, inputs, specs, [like((height, depth), dtype)], [out_spec], (depth // tile,)
        )[0]

    held, totals, turned_left = [], [], []

    def chunk(index, first, width):
        parts = ((0, 1), (1, n_sum))
        yield "pack first"
        packed = [swap(pack(first, width, *parts[0]))]
        yield "pack"
        packed.append(swap(pack(first, width, *parts[1])))
        yield "right first"
        blocks = list(right(packed[0], first, width, *parts[0]))
        early = along(blocks[0], streams(spots, False)[0][2])
        if index == 0:
            turned_left.append(turn())
        yield "right"
        blocks += right(packed[1], first, width, *parts[1])
        got = {}
        for t, parity, pairs in sorted(streams(spots, False), key=lambda x: x[:2]):
            value = blocks[sum_slot[t, parity]]
            before = got.get((t - 1, 1 - parity))
            if before is not None:
                yield f"sum {t} {parity}"
                value = add(value, before)
            got[t, parity] = along(value, pairs) if got else early
        yield "left"
        sums = left_sums([blocks[n_sum - 1]] + [got[k] for k in got if k[0] == spots - 2])
        if square:
            keep, by_x, by_y, then_y, then_x = sums
            got_x, got_y = to_partner(by_x, 1), to_partner(by_y, 2)
            yield "fold"
            then_y, then_x = fold(then_y, got_x, then_x, got_y)
            last_y, last_x = to_partner(then_y, 2), to_partner(then_x, 1)
            parts = [keep, [(got_x, 0), (got_y, 0)], [(last_y, None), (last_x, None)]]
        else:
            parts = across(sums)
        yield "moments"
        upper, lower = moments(parts, first, width)
        if square:
            upper_y, lower_x = to_partner(upper, 2), to_partner(lower, 1)
            yield "unfold"
            uppers, lowers = unfold(upper, upper_y, lower, lower_x)
            by_x, by_y = to_partner(uppers, 1), to_partner(lowers, 2)
            steps = [
                [(upper, None), (lower, None)],
                [(by_x, 0), (lower_x, None)],
                [(upper_y, None), (by_y, 0)],
                [(by_x, 1), (by_y, 1)],
            ]
        else:
            steps = [[(x, None)] for x in spread(jnp.concatenate([upper, lower]))]
        yield "back"
        turned = left_times(steps)
        got = {}
        for t, parity, pairs in streams(spots, True):
            value = turned
            if t:
                before = (t - 1, 1 - parity)
                yield f"pass {t} {parity}"
                value = hand_on(got[before], [got[t - 1, parity]] if t > 1 and (t - 1, parity) in got else [])
                got[before] = value
            got[t, parity] = along(value, pairs)
        held.append((first, width, packed, [[turned]] + [[got[k] for k in group] for group in groups]))
        last = index == len(widths) - 1
        if index < len(widths) - 2:
            return
        if not last:
            yield "away"
            away = swap(back(held[: index + 1], False, BF16))
            totals.append(away)
        else:
            yield "near"
            half = n_gather - 1
            most = back(held[-1:], True, F32, (), True, range(half))
            if index:
                totals.append(back(held[:-1], True, F32, [most]))
            else:
                totals.append(most)
            yield "end"
            final = held[-1][3][-1]
            final[:] = [hand_on(x) for x in final]
            totals[:] = [back(held[-1:], True, F32, totals, True, range(half, n_gather))]

    run(spots == 4, [chunk(k, first, width) for k, (first, width) in enumerate(widths)])
    return (kept[0], kept[1], totals[0])


def solution(mesh):
    row_size, col_size = mesh.shape["row"], mesh.shape["col"]

    def whole(gradient, *rest):
        columns = gradient.shape[1] // col_size
        width = columns // 2
        widths = [(first, width) for first in range(0, columns, width)]
        return jax.shard_map(
            functools.partial(body, row_size, col_size, widths),
            mesh=mesh,
            in_specs=(
                P("row", "col"),
                P("row", None),
                P("col", None),
                P("row", "col"),
                P("row", "col"),
            ),
            out_specs=(P("row", "col"), P("row", "col"), P("row", "col")),
            check_vma=False,
        )(gradient, *rest)

    return whole
```

```python
import functools

import jax
import jax.numpy as jnp
import numpy as np
from jax import lax
from jax.experimental import pallas as pl
from jax.experimental.pallas import tpu as pltpu
from jax.sharding import PartitionSpec as P

F32, BF16 = jnp.float32, jnp.bfloat16
VMEM_BYTES = 39 * 2**20
FLOPS_A_US = 7 * 10**9
ANY = pl.BlockSpec(memory_space=pl.ANY)


def like(shape, dtype):
    return jax.ShapeDtypeStruct(tuple(shape), dtype)


class Order:
    def __init__(self):
        self.last = None

    def call(self, us, kernel, place, inputs, in_specs, outs, out_specs, grid, aliases=None):
        n_in = len(inputs)
        extra = [] if self.last is None else [self.last]

        def wrapped(place_ref, *refs):
            kernel(place_ref, refs[:n_in], refs[n_in + len(extra) :])

        got = pl.pallas_call(
            wrapped,
            out_shape=outs,
            grid_spec=pltpu.PrefetchScalarGridSpec(
                num_scalar_prefetch=1,
                grid=grid,
                in_specs=list(in_specs) + [ANY] * len(extra),
                out_specs=out_specs,
            ),
            input_output_aliases={k + 1: v for k, v in (aliases or {}).items()},
            compiler_params=pltpu.CompilerParams(vmem_limit_bytes=VMEM_BYTES),
            cost_estimate=pl.CostEstimate(flops=int(us * FLOPS_A_US), bytes_accessed=1, transcendentals=0),
        )(place, *inputs, *extra)
        self.last = got[0]
        return got


def streams(spots, gather):
    out = []
    for t in range(spots - 1):
        for parity in range(2):
            edges = range(parity, spots - 1, 2)
            if gather:
                pairs = [(e, e + 1) for e in edges if e >= t]
                pairs += [(e + 1, e) for e in edges if e + 1 <= spots - 1 - t]
            else:
                pairs = [(e, e + 1) for e in edges if e <= t]
                pairs += [(e + 1, e) for e in edges if e >= spots - 2 - t]
            if pairs:
                out.append((t, parity, pairs))
    return out


def slots_of(spots, gather):
    groups, users, slot, table = [], [], {}, []
    for t, parity, pairs in streams(spots, gather):
        who = {}
        for a, b in pairs:
            if gather:
                who[b] = b - (t + 1) if a < b else b + (t + 1)
            else:
                who[a] = a + (spots - 1 - t) if a < b else a - (spots - 1 - t)
        for k in range(len(groups) + 1):
            if k == len(groups):
                groups.append([])
                users.append({})
            if not set(users[k]) & set(who):
                break
        groups[k].append((t, parity))
        users[k].update(who)
        slot[t, parity] = k
    table = [[users[k].get(z, 0) for k in range(len(groups))] for z in range(spots)]
    return groups, slot, np.array(table, np.int32)


STEPS = {
    "pack first": -24.0,
    "pack": -20.0,
    "right first": -16.0,
    "right": -4.0,
    "sum 1 1": 20.0,
    "sum 2 1": 37.0,
    "sum 2 0": 41.0,
    "left": 62.0,
    "fold": 88.0,
    "moments": 101.0,
    "unfold": 117.0,
    "back": 138.0,
    "pass 1 0": 163.1,
    "pass 1 1": 163.0,
    "pass 2 0": 184.0,
    "away": 205.0,
    "near": 186.0,
}
APART = 58.0


def nominal(step, index):
    if step == "end":
        return 1e6
    if step in STEPS:
        return STEPS[step] + APART * index
    kind, t, _ = step.split()
    return STEPS["left" if kind == "sum" else "pass 2 0"] - 1.0 / (1 + int(t)) + APART * index


TURNS = "000010100110101100101100101011111"


def run(short, tasks):
    waiting = {k: next(task) for k, task in enumerate(tasks)}
    turns = [int(k) for k in TURNS] if short else []
    while waiting:
        k = min(waiting, key=lambda k: (nominal(waiting[k], k), k))
        if turns:
            k = turns.pop(0)
        try:
            waiting[k] = next(tasks[k])
        except StopIteration:
            del waiting[k]


def body(row_size, col_size, widths, gradient, left_basis, right_basis, first_moment, second_moment):
    height, columns = first_moment.shape
    spots = col_size // 2
    col, row = lax.axis_index("col"), lax.axis_index("row")
    at, core = col // 2, col % 2
    direct, square = row_size in (2, 4), row_size == 4
    slots = np.arange(row_size, dtype=np.int32)

    _, sum_slot, sum_table = slots_of(spots, False)
    groups, gather_slot, gather_table = slots_of(spots, True)
    n_sum, n_gather = sum_table.shape[1] + 1, gather_table.shape[1] + 1
    own = np.arange(spots, dtype=np.int32)[:, None]
    sum_table = np.concatenate([sum_table, own], 1)
    gather_table = np.concatenate([own, gather_table], 1)
    same = np.array(
        [[list(sum_table[z]).index(d) for d in gather_table[z]] for z in range(spots)], np.int32
    )
    table = np.concatenate([sum_table, gather_table, same], 1)
    place = jnp.concatenate(
        [
            core.astype(jnp.int32).reshape(1),
            (slots ^ row.astype(jnp.int32)) if direct else jnp.asarray(slots),
            jnp.asarray(table)[at],
        ]
    )
    at_row, at_sum = 1, 1 + row_size
    at_gather, at_same = at_sum + n_sum, at_sum + n_sum + n_gather

    order = Order()

    def swap(x):
        return lax.ppermute(x, "col", [(j, j ^ 1) for j in range(col_size)])

    def along(x, pairs):
        return lax.ppermute(x, "col", [(2 * a + c, 2 * b + c) for a, b in pairs for c in range(2)])

    def to_partner(x, s):
        return lax.ppermute(x, "row", [(i, i ^ s) for i in range(row_size)])

    def across(blocks):
        if not direct:
            return [lax.psum_scatter(jnp.concatenate(blocks), "row", scatter_dimension=0, tiled=True)]
        return [blocks[0]] + [
            to_partner(blocks[s], s) for s in range(1, row_size)
        ]

    def spread(block):
        if not direct:
            whole = lax.all_gather(block, "row", axis=0, tiled=False)
            return [whole[s] for s in range(row_size)]
        return across([block] * row_size)

    other_gradient = swap(gradient)

    def turn():
        def kernel(_, ins, outs):
            outs[0][...] = ins[0][...].T

        return order.call(
            4.0,
            kernel,
            place,
            [left_basis],
            [pl.BlockSpec((height, height), lambda s, p: (0, p[at_row + s]))],
            [like((row_size * height, height), BF16)],
            [pl.BlockSpec((height, height), lambda s, p: (s, 0))],
            (row_size,),
        )[0]

    def pack(first, width, low, high):
        stride = columns // width

        def kernel(_, ins, outs):
            outs[0][0] = ins[0][...]

        depth = right_basis.shape[0]
        return order.call(
            1.5 * (high - low),
            kernel,
            place,
            [right_basis],
            [
                pl.BlockSpec(
                    (depth, width),
                    lambda s, p: (0, (2 * p[at_sum + low + s] + 1 - p[0]) * stride + first // width),
                )
            ],
            [like((high - low, depth, width), BF16)],
            [pl.BlockSpec((1, depth, width), lambda s, p: (s, 0, 0))],
            (high - low,),
        )[0]

    def right(packed, first, width, low, high):
        stride = columns // width
        depth = right_basis.shape[0]

        def kernel(_, ins, outs):
            mine, theirs, basis, other = ins
            value = jnp.dot(mine[...], basis[...], preferred_element_type=F32)
            value += jnp.dot(theirs[...], other[0], preferred_element_type=F32)
            value = value.astype(BF16)
            for s in range(high - low):

                @pl.when(pl.program_id(0) == s)
                def _(s=s):
                    outs[s][...] = value

        whole = pl.BlockSpec((height, depth), lambda s, p: (0, 0))
        return order.call(
            2.5 * (high - low),
            kernel,
            place,
            [gradient, other_gradient, right_basis, packed],
            [
                whole,
                whole,
                pl.BlockSpec(
                    (depth, width),
                    lambda s, p: (0, (2 * p[at_sum + low + s] + p[0]) * stride + first // width),
                ),
                pl.BlockSpec((1, depth, width), lambda s, p: (s, 0, 0)),
            ],
            [like((height, width), BF16)] * (high - low),
            [pl.BlockSpec((height, width), lambda s, p: (0, 0))] * (high - low),
            (high - low,),
        )

    def add(x, y):
        def kernel(_, ins, outs):
            outs[0][...] = (ins[0][...].astype(F32) + ins[1][...].astype(F32)).astype(BF16)

        spec = pl.BlockSpec(x.shape, lambda s, p: (0, 0))
        return order.call(2.0, kernel, place, [x, y], [spec, spec], [like(x.shape, BF16)], [spec], (1,))[0]

    def hand_on(x, also=()):
        def kernel(_, ins, outs):
            pass

        return order.call(
            0.5,
            kernel, place, [x, *also], [ANY] * (1 + len(also)), [like(x.shape, BF16)], [ANY], (1,), {0: 0}
        )[0]

    def left_sums(terms):
        width = terms[0].shape[1]
        n = len(terms)
        half = height // 2

        def kernel(_, ins, outs):
            total = ins[0][...].astype(F32)
            for term in ins[1:n]:
                total += term[...].astype(F32)
            value = jnp.dot(ins[n][...], total.astype(BF16), preferred_element_type=F32).astype(BF16)
            for s in range(row_size):

                @pl.when(pl.program_id(0) == s)
                def _(s=s):
                    if not square:
                        outs[s][...] = value
                        return
                    keep, by_x, by_y, then_y, then_x = outs
                    if s == 0:
                        keep[...] = value
                    if s & 1:
                        by_x[s // 2] = value[:half]
                    if s & 2:
                        by_y[s - 2] = value[half:]
                    if s == 2:
                        then_y[...] = value[:half]
                    if s == 1:
                        then_x[...] = value[half:]

        spec = pl.BlockSpec((height, width), lambda s, p: (0, 0))
        if square:
            shapes = [(height, width), (2, half, width), (2, half, width), (half, width), (half, width)]
        else:
            shapes = [(height, width)] * row_size
        return order.call(
            5.0,
            kernel,
            place,
            [*terms, turned_left[0]],
            [spec] * n + [pl.BlockSpec((height, height), lambda s, p: (s, 0))],
            [like(shape, BF16) for shape in shapes],
            [pl.BlockSpec(shape, lambda s, p, zeros=(0,) * len(shape): zeros) for shape in shapes],
            (row_size,),
        )

    def whole_spec(x):
        return pl.BlockSpec(x.shape, lambda s, p, zeros=(0,) * x.ndim: zeros)

    def fold(then_y, got_x, then_x, got_y):
        def kernel(_, ins, outs):
            for k in range(2):
                outs[k][...] = (ins[2 * k][...].astype(F32) + ins[2 * k + 1][1].astype(F32)).astype(BF16)

        inputs = [then_y, got_x, then_x, got_y]
        outs = [like(then_y.shape, BF16)] * 2
        return order.call(
            1.0,
            kernel, place, inputs, [whole_spec(x) for x in inputs], outs, [whole_spec(x) for x in outs], (1,)
        )

    def unfold(upper, got_upper, lower, got_lower):
        def kernel(_, ins, outs):
            for k in range(2):
                outs[k][0] = ins[2 * k][...]
                outs[k][1] = ins[2 * k + 1][...]

        inputs = [upper, got_upper, lower, got_lower]
        outs = [like((2, *upper.shape), BF16)] * 2
        return order.call(
            1.5,
            kernel, place, inputs, [whole_spec(x) for x in inputs], outs, [whole_spec(x) for x in outs], (1,)
        )

    def left_times(blocks):
        width = blocks[0][0][0].shape[-1]
        tile = height // 3 if height % 48 == 0 else height
        inputs, layout = [], []
        for views in blocks:
            refs = []
            for x, k in views:
                n = next((n for n, y in enumerate(inputs) if x is y), len(inputs))
                if n == len(inputs):
                    inputs.append(x)
                refs.append((n, k))
            layout.append(refs)
        first = len(inputs)

        def kernel(_, ins, outs):
            total = 0.0
            for s, refs in enumerate(layout):
                parts = [ins[n][...] if k is None else ins[n][k] for n, k in refs]
                x = parts[0] if len(parts) == 1 else jnp.concatenate(parts, axis=0)
                total += jnp.dot(ins[first + s][...], x, preferred_element_type=F32)
            outs[0][...] = total.astype(BF16)

        return order.call(
            5.0,
            kernel,
            place,
            [*inputs, *([left_basis] * row_size)],
            [whole_spec(x) for x in inputs]
            + [
                pl.BlockSpec((tile, height), lambda r, p, s=s: (r, p[at_row + s]))
                for s in range(row_size)
            ],
            [like((height, width), BF16)],
            [pl.BlockSpec((tile, width), lambda r, p: (r, 0))],
            (height // tile,),
        )[0]

    kept = []

    def moments(parts, first, width):
        tile = height // 4 if height % 64 == 0 else height // 2
        per_half = height // 2 // tile
        first_fix = 1.0 - 0.9**20
        second_fix = 1.0 - 0.95**20
        inputs, specs, halves = [], [], [[], []]
        for part in parts:
            if not isinstance(part, list):
                for k in range(2):
                    halves[k].append(len(inputs))
                inputs.append(part)
                specs.append(pl.BlockSpec((tile, width), lambda r, p: (r, 0)))
                continue
            for k, (x, at_x) in enumerate(part):
                halves[k].append(len(inputs))
                inputs.append(x)
                low = k * per_half

                def at(r, p, low=low, at_x=at_x):
                    r = jnp.clip(r - low, 0, per_half - 1)
                    return (r, 0) if at_x is None else (at_x, r, 0)

                specs.append(pl.BlockSpec((tile, width) if at_x is None else (None, tile, width), at))
        n = len(inputs)

        def kernel(_, ins, outs):
            for k in range(2):

                @pl.when(pl.program_id(0) // per_half == k)
                def _(k=k):
                    rotated = sum(ins[m][...].astype(F32) for m in halves[k])
                    nf = 0.9 * ins[n][...] + 0.1 * rotated
                    ns = 0.95 * ins[n + 1][...] + 0.05 * rotated * rotated
                    outs[2][...] = nf
                    outs[3][...] = ns
                    outs[k][...] = (nf * (1.0 / first_fix) / (jnp.sqrt(ns * (1.0 / second_fix)) + 1e-08)).astype(BF16)

        spot = pl.BlockSpec((tile, width), lambda r, p: (r, first // width))
        half_specs = [
            pl.BlockSpec((tile, width), lambda r, p, k=k: (jnp.clip(r - k * per_half, 0, per_half - 1), 0))
            for k in range(2)
        ]
        upper, lower, *kept[:] = order.call(
            5.0,
            kernel,
            place,
            [*inputs, first_moment, second_moment, *kept],
            specs + [spot, spot] + [ANY] * len(kept),
            [like((height // 2, width), BF16)] * 2 + [like((height, columns), F32)] * 2,
            [*half_specs, spot, spot],
            (height // tile,),
            {n + 2: 2, n + 3: 3} if kept else None,
        )
        return upper, lower

    def back(chunks, mine, dtype, ends=(), both=False, some=None):
        depth = right_basis.shape[0]
        tile = min(256, depth)
        inputs, specs, layout, at_g = [], [], [], []
        whole = [pl.BlockSpec((height, width), lambda r, p: (0, 0)) for _, width, _, _ in chunks]
        for at_chunk, (first, width, packed, gathered) in enumerate(chunks):
            stride = columns // width
            for flip in range(2 if both else 1):
                for g in range(n_gather) if some is None else some:
                    xs = [swap(x) for x in gathered[g]] if flip else gathered[g]
                    inputs += xs
                    specs += [whole[at_chunk]] * len(xs)
                    layout.append(len(xs))
                    at_g.append(g)
                    if mine:

                        def at(r, p, g=g, flip=flip, stride=stride, first=first, width=width):
                            half = p[0] if flip == 0 else 1 - p[0]
                            return (r, (2 * p[at_gather + g] + half) * stride + first // width)

                        inputs.append(right_basis)
                        specs.append(pl.BlockSpec((tile, width), at))
                    else:
                        for k, x in enumerate(packed):
                            low, high = (0, 1) if k == 0 else (1, n_sum)

                            def at_packed(r, p, g=g, low=low, high=high):
                                return (jnp.clip(p[at_same + g] - low, 0, high - low - 1), r, 0)

                            inputs.append(x)
                            specs.append(pl.BlockSpec((1, tile, width), at_packed))
        out_spec = pl.BlockSpec((height, tile), lambda r, p: (0, r))
        n = len(inputs)
        inputs += list(ends)
        specs += [out_spec] * len(ends)

        def kernel(p_ref, ins, outs):
            total = jnp.zeros((height, tile), F32)
            k = 0
            for j, count in enumerate(layout):
                x = ins[k][...]
                for more in ins[k + 1 : k + count]:
                    x = x + more[...]
                if mine:
                    basis = ins[k + count][...]
                else:
                    basis = jnp.where(p_ref[at_same + at_g[j]] == 0, ins[k + count][0], ins[k + count + 1][0])
                total += lax.dot_general(x, basis, (((1,), (1,)), ((), ())), preferred_element_type=F32)
                k += count + (1 if mine else 2)
            for end in ins[n:]:
                total += end[...].astype(F32)
            outs[0][...] = total.astype(dtype)

        return order.call(
            8.0,
            kernel, place, inputs, specs, [like((height, depth), dtype)], [out_spec], (depth // tile,)
        )[0]

    held, totals, turned_left = [], [], []

    def chunk(index, first, width):
        parts = ((0, 1), (1, n_sum))
        yield "pack first"
        packed = [swap(pack(first, width, *parts[0]))]
        yield "pack"
        packed.append(swap(pack(first, width, *parts[1])))
        yield "right first"
        blocks = list(right(packed[0], first, width, *parts[0]))
        early = along(blocks[0], streams(spots, False)[0][2])
        if index == 0:
            turned_left.append(turn())
        yield "right"
        blocks += right(packed[1], first, width, *parts[1])
        got = {}
        for t, parity, pairs in sorted(streams(spots, False), key=lambda x: x[:2]):
            value = blocks[sum_slot[t, parity]]
            before = got.get((t - 1, 1 - parity))
            if before is not None:
                yield f"sum {t} {parity}"
                value = add(value, before)
            got[t, parity] = along(value, pairs) if got else early
        yield "left"
        sums = left_sums([blocks[n_sum - 1]] + [got[k] for k in got if k[0] == spots - 2])
        if square:
            keep, by_x, by_y, then_y, then_x = sums
            got_x, got_y = to_partner(by_x, 1), to_partner(by_y, 2)
            yield "fold"
            then_y, then_x = fold(then_y, got_x, then_x, got_y)
            last_y, last_x = to_partner(then_y, 2), to_partner(then_x, 1)
            parts = [keep, [(got_x, 0), (got_y, 0)], [(last_y, None), (last_x, None)]]
        else:
            parts = across(sums)
        yield "moments"
        upper, lower = moments(parts, first, width)
        if square:
            upper_y, lower_x = to_partner(upper, 2), to_partner(lower, 1)
            yield "unfold"
            uppers, lowers = unfold(upper, upper_y, lower, lower_x)
            by_x, by_y = to_partner(uppers, 1), to_partner(lowers, 2)
            steps = [
                [(upper, None), (lower, None)],
                [(by_x, 0), (lower_x, None)],
                [(upper_y, None), (by_y, 0)],
                [(by_x, 1), (by_y, 1)],
            ]
        else:
            steps = [[(x, None)] for x in spread(jnp.concatenate([upper, lower]))]
        yield "back"
        turned = left_times(steps)
        got = {}
        for t, parity, pairs in streams(spots, True):
            value = turned
            if t:
                before = (t - 1, 1 - parity)
                yield f"pass {t} {parity}"
                value = hand_on(got[before], [got[t - 1, parity]] if t > 1 and (t - 1, parity) in got else [])
                got[before] = value
            got[t, parity] = along(value, pairs)
        held.append((first, width, packed, [[turned]] + [[got[k] for k in group] for group in groups]))
        last = index == len(widths) - 1
        if index < len(widths) - 2:
            return
        if not last:
            yield "away"
            away = swap(back(held[: index + 1], False, BF16))
            totals.append(away)
        else:
            yield "near"
            half = n_gather - 1
            most = back(held[-1:], True, F32, (), True, range(half))
            if index:
                totals.append(back(held[:-1], True, F32, [most]))
            else:
                totals.append(most)
            yield "end"
            final = held[-1][3][-1]
            final[:] = [hand_on(x) for x in final]
            totals[:] = [back(held[-1:], True, F32, totals, True, range(half, n_gather))]

    run(spots == 4, [chunk(k, first, width) for k, (first, width) in enumerate(widths)])
    return (kept[0], kept[1], totals[0])


def solution(mesh):
    row_size, col_size = mesh.shape["row"], mesh.shape["col"]

    def whole(gradient, *rest):
        columns = gradient.shape[1] // col_size
        width = columns // 2
        widths = [(first, width) for first in range(0, columns, width)]
        return jax.shard_map(
            functools.partial(body, row_size, col_size, widths),
            mesh=mesh,
            in_specs=(
                P("row", "col"),
                P("row", None),
                P("col", None),
                P("row", "col"),
                P("row", "col"),
            ),
            out_specs=(P("row", "col"), P("row", "col"), P("row", "col")),
            check_vma=False,
        )(gradient, *rest)

    return whole
```
